32 devices in a mesh: groups: 1, tensor: 32 (over z, y, x, core).
Axes of the slice: x: 2, y: 2, z: 4, core: 2. Of those that a mesh axis runs over, the one named last changes fastest.
Arguments:
- query_grads: bfloat16 [2, 4096, 16384], P('groups', 'tensor'), may hold values from -0.0007324219 to 0.0007324219
- eigen_values: float32 [4096, 16384], P('groups', 'tensor'), may hold values from 0.1 to 10
- act_basis: bfloat16 [128, 128, 128], P(('groups', 'tensor')), may hold values from -0.5 to 0.5
- grad_basis: bfloat16 [4096, 256], P(('groups', 'tensor')), may hold values from -0.375 to 0.375
- activations: bfloat16 [256, 16384], P(('groups', 'tensor')), may hold values from -6 to 6
- cotangents: bfloat16 [256, 4096], P(('groups', 'tensor')), may hold values from -6 to 6
- block_tokens: int32 [256], P('groups'), may hold values from 0 to 255, each once
- pair_query: int32 [24], P('groups'), may hold values from 0 to 1
- pair_block: int32 [24], P('groups'), may hold values from 0 to 1
Outputs:
- scores: float32 [24, 128], P('groups')
The draws below stay inside these ranges and needn't reach their ends.
Inputs may be any that keep to these rules, and one draw needn't show every extreme that they name: `block_tokens`: a permutation of the training tokens.
All inputs are finite; a program needn't handle non-finite values.
Results may differ from the reference program's by a relative error of at most 0.005.
Values may be sent and summed in bfloat16 or wider, within the bound.
A program may use at most 128 MiB of HBM per device.

```python
import math
import jax
import jax.numpy as jnp
import numpy as np
from jax import lax

FFW = 16384
DW = 4096
AB = 128
GB = 256
BLOCK = 128
QRY = 2
PAIRS = 24
TOK = 256
NB = 2


def plant(drawn, rng, smallest, high):
    spot = [jax.random.randint(jax.random.fold_in(rng, axis), (), 0, length) for axis, length in enumerate(drawn.shape)]
    main_axis = drawn.shape.index(max(drawn.shape))
    next_to = spot[:main_axis] + [(spot[main_axis] + 1) % drawn.shape[main_axis]] + spot[main_axis + 1:]
    return drawn.at[tuple(spot)].set(smallest).at[tuple(next_to)].set(high)


def level_of(stream_key, dims, shards, smallest, largest):
    def one(position, parts):
        steps = jax.random.uniform(jax.random.fold_in(jax.random.fold_in(stream_key, 6), position), (parts,), jnp.float32, smallest / len(shards), largest / len(shards))
        return jnp.repeat(jnp.exp(steps), dims[position] // parts).reshape((-1,) + (1,) * (len(dims) - position - 1))

    loudness = one(*shards[0])
    for cut in shards[1:]:
        loudness = loudness * one(*cut)
    return loudness


def rank_bounds(count, skew):
    weights = [(1 << 20) // math.isqrt(standing ** skew) + 1 for standing in range(1, count + 1)]
    scale = 1 + sum(weights) // (1 << 30)
    return np.cumsum(np.array([max(1, weight // scale) for weight in weights]))


def skewed_ids(key, extent, amount, skew):
    listing = rank_bounds(amount, skew)
    pick = jax.random.randint(jax.random.fold_in(key, 1), extent, 0, int(listing[amount - 1]))
    grade = jnp.searchsorted(jnp.asarray(listing, jnp.int32), pick, side="right")
    return jax.random.permutation(jax.random.fold_in(key, 2), amount)[grade].astype(jnp.int32)


def noise(own_key, shape, width, reach, shards=(), kind=jnp.bfloat16):
    level = level_of(own_key, shape, shards, -0.22, 0.18) if shards else 1.0
    drawn = jax.random.normal(own_key, shape, jnp.float32) * width * level
    return jnp.minimum(jnp.maximum(drawn, -reach), reach).astype(kind)


def setup_inputs(seed: int = 0, part: int = 0) -> dict:
    seeds = jax.random.split(jax.random.key(seed), 10)
    part_splits = jax.random.split(jax.random.fold_in(seeds[9], part), 10)
    return {
        "query_grads": noise(part_splits[0], (QRY, DW, FFW), (DW * FFW) ** -0.5, 0.0007324219, ((1, 32),)),
        "eigen_values": jnp.clip(jnp.exp(math.log(10.0) - 4.6051702 * jax.random.uniform(part_splits[1], (DW, FFW), jnp.float32) ** level_of(part_splits[1], (DW, FFW), ((1, 32),), -0.2, 0.2)), 0.1, 10.0),
        "act_basis": noise(part_splits[2], (FFW // AB, AB, AB), AB ** -0.5, 0.5, ((0, 32),)),
        "grad_basis": noise(part_splits[3], (DW, GB), GB ** -0.5, 0.375, ((0, 32),)),
        "activations": noise(part_splits[4], (TOK, FFW), 1.0, 6.0, ((0, 32),)),
        "cotangents": noise(part_splits[5], (TOK, DW), 1.0, 6.0, ((0, 32),)),
        "block_tokens": jax.random.permutation(part_splits[6], TOK).astype(jnp.int32),
        "pair_query": plant(jax.random.randint(part_splits[7], (PAIRS,), 0, QRY), jax.random.fold_in(part_splits[7], 1), 0, QRY - 1).astype(jnp.int32),
        "pair_block": plant(skewed_ids(part_splits[8], (PAIRS,), NB, 2), jax.random.fold_in(part_splits[8], 3), 0, NB - 1).astype(jnp.int32),
    }


damping = 0.1


def reference(query_grads, eigen_values, act_basis, grad_basis, activations, cotangents, block_tokens, pair_query, pair_block):
    act_blocks = act_basis.astype(jnp.float32)
    grad_blocks = grad_basis.reshape(DW // GB, GB, GB).astype(jnp.float32)

    def precondition(query):
        turned = jnp.einsum("okb,kbc->okc", query.reshape(DW, FFW // AB, AB).astype(jnp.float32), act_blocks)
        turned = turned.astype(jnp.bfloat16).reshape(DW // GB, GB, FFW).astype(jnp.float32)
        rotated = jnp.einsum("cgh,cgf->chf", grad_blocks, turned).reshape(DW, FFW)
        return (rotated / (eigen_values + damping)).astype(jnp.bfloat16)

    precond = lax.map(precondition, query_grads)
    act_rot = jnp.einsum("tkb,kbc->tkc", activations.reshape(TOK, FFW // AB, AB).astype(jnp.float32), act_blocks)
    act_rot = act_rot.astype(jnp.bfloat16).reshape(TOK, FFW)
    cot_rot = jnp.einsum("tcg,cgh->tch", cotangents.reshape(TOK, DW // GB, GB).astype(jnp.float32), grad_blocks)
    cot_rot = cot_rot.astype(jnp.bfloat16).reshape(TOK, DW)
    blocks = block_tokens.reshape(NB, BLOCK)

    def score_pair(members):
        query_index, block_index = members
        token_ids = blocks[block_index]
        grad_rows = jnp.take(cot_rot, token_ids, axis=0)
        act_rows = jnp.take(act_rot, token_ids, axis=0)
        products = jnp.dot(grad_rows, precond[query_index], preferred_element_type=jnp.float32)
        return jnp.sum(products * act_rows.astype(jnp.float32), axis=1)

    return lax.map(score_pair, (pair_query, pair_block))
```

```python
import jax
import jax.numpy as jnp
from jax import lax
from jax.sharding import PartitionSpec as P

BLOCK = 128


damping = 0.1


def rotate_rows(rows, grad_blocks):
    row_count = rows.shape[0]
    nblocks = grad_blocks.shape[0]
    block_width = grad_blocks.shape[1]
    reshaped = rows.reshape(row_count, nblocks, block_width)
    turned = jnp.einsum("tcg,cgh->tch", reshaped, grad_blocks, preferred_element_type=jnp.float32)
    return turned.astype(jnp.bfloat16).reshape(row_count, nblocks * block_width)


def pick_scores(totals, block_tokens, pair_query, pair_block):
    blocks = block_tokens.reshape(-1, BLOCK)
    picked = jnp.take(totals, pair_query, axis=0)
    token_ids = jnp.take(blocks, pair_block, axis=0)
    return jnp.take_along_axis(picked, token_ids, axis=1)


def by_columns(
    query_grads,
    eigen_values,
    act_basis,
    grad_basis,
    activations,
    cotangents,
    block_tokens,
    pair_query,
    pair_block,
):
    grad_full = lax.all_gather(grad_basis, "tensor", axis=0, tiled=True)
    block_width = grad_full.shape[1]
    model_cols = grad_full.shape[0]
    grad_blocks = grad_full.reshape(model_cols // block_width, block_width, block_width)
    act_local = lax.all_to_all(activations, "tensor", split_axis=1, concat_axis=0, tiled=True)
    tokens_all = act_local.shape[0]
    slice_cols = act_local.shape[1]
    owned_blocks = act_basis.shape[0]
    act_size = act_basis.shape[1]
    act_rot = jnp.einsum(
        "tkb,kbc->tkc",
        act_local.reshape(tokens_all, owned_blocks, act_size),
        act_basis,
        preferred_element_type=jnp.float32,
    )
    act_rot = act_rot.astype(jnp.bfloat16).reshape(tokens_all, slice_cols)
    cot_mine = rotate_rows(cotangents, grad_blocks)
    cot_rot = lax.all_gather(cot_mine, "tensor", axis=0, tiled=True)
    query_piece = lax.all_to_all(query_grads, "tensor", split_axis=2, concat_axis=1, tiled=True)
    number = query_piece.shape[0]
    turned = jnp.einsum(
        "nokb,kbc->nokc",
        query_piece.reshape(number, model_cols, owned_blocks, act_size),
        act_basis,
        preferred_element_type=jnp.float32,
    ).astype(jnp.bfloat16)
    turned = turned.reshape(number, model_cols // block_width, block_width, slice_cols)
    rotated = jnp.einsum("cgh,ncgf->nchf", grad_blocks, turned, preferred_element_type=jnp.float32)
    rotated = rotated.reshape(number, model_cols, slice_cols)
    precond = (rotated / (eigen_values + damping)).astype(jnp.bfloat16)
    act_wide = act_rot.astype(jnp.float32)

    def score_query(matrix):
        values = jnp.dot(cot_rot, matrix, preferred_element_type=jnp.float32)
        return jnp.sum(values * act_wide, axis=1)

    totals = lax.map(score_query, precond)
    return lax.psum(pick_scores(totals, block_tokens, pair_query, pair_block), "tensor")


def by_rows(
    query_grads,
    eigen_values,
    act_basis,
    grad_basis,
    activations,
    cotangents,
    block_tokens,
    pair_query,
    pair_block,
):
    devices = lax.axis_size("tensor")
    chips = devices // 2
    across = [[2 * chip + core for chip in range(chips)] for core in range(2)]
    pairs = [[2 * chip, 2 * chip + 1] for chip in range(chips)]
    bf16, f32 = jnp.bfloat16, jnp.float32

    number, rows, hidden = query_grads.shape
    width = eigen_values.shape[1]
    wide = 2 * rows
    half = hidden // 2
    tokens = activations.shape[0]

    inverse = (1.0 / (eigen_values + damping)).astype(bf16)
    inverse = lax.all_to_all(inverse, "tensor", 0, 1, axis_index_groups=across, tiled=True)
    basis = lax.all_gather(act_basis, "tensor", axis=0, axis_index_groups=across, tiled=True)
    act = activations.reshape(tokens, chips, 2, width)
    act = lax.all_to_all(act, "tensor", 2, 0, axis_index_groups=pairs, tiled=True)
    act = act.reshape(2 * tokens, half)
    act = lax.all_gather(act, "tensor", axis=0, axis_index_groups=across, tiled=True)
    query = query_grads.reshape(number, rows, chips, 2, width)
    query = lax.all_to_all(query, "tensor", 3, 1, axis_index_groups=pairs, tiled=True)
    grad = lax.all_gather(grad_basis, "tensor", axis=0, axis_index_groups=pairs, tiled=True)
    cot = lax.all_to_all(cotangents, "tensor", 1, 0, axis_index_groups=across, tiled=True)
    cot = lax.all_gather(cot, "tensor", axis=0, axis_index_groups=pairs)
    cot = cot.reshape(2, chips, tokens, wide).transpose(1, 0, 2, 3).reshape(devices * tokens, wide)

    cot_rot = jnp.dot(cot, grad, preferred_element_type=f32).astype(bf16)
    blocks, size, _ = basis.shape
    act_rot = jnp.einsum("tkb,kbc->tkc", act.reshape(-1, blocks, size), basis, preferred_element_type=f32)
    act_rot = act_rot.astype(bf16).reshape(-1, half)
    turned = jnp.einsum(
        "nokb,kbc->nokc", query.reshape(number, wide, blocks, size), basis, preferred_element_type=f32
    )
    turned = turned.astype(bf16).reshape(number, wide, half)
    rotated = jnp.einsum("gh,ngf->nhf", grad, turned, preferred_element_type=f32)
    precond = (rotated * inverse.astype(f32)).astype(bf16)
    values = jnp.einsum("tf,nhf->nth", act_rot, precond, preferred_element_type=f32)
    totals = jnp.sum(values * cot_rot.astype(f32), axis=2)
    return pick_scores(lax.psum(totals, "tensor"), block_tokens, pair_query, pair_block)


def solution(mesh):
    devices = mesh.shape["tensor"]

    def per_device(*args):
        query_grads, grad_basis = args[0], args[3]
        paired = devices % 2 == 0 and 2 * query_grads.shape[1] == grad_basis.shape[1]
        return (by_rows if paired else by_columns)(*args)

    return jax.shard_map(
        per_device,
        mesh=mesh,
        in_specs=(
            P("groups", "tensor", None),
            P("groups", "tensor"),
            P(("groups", "tensor"), None, None),
            P(("groups", "tensor"), None),
            P(("groups", "tensor"), None),
            P(("groups", "tensor"), None),
            P("groups"),
            P("groups"),
            P("groups"),
        ),
        out_specs=P("groups", None),
        check_vma=False,
    )
```

```python
import jax
import jax.numpy as jnp
from jax import lax
from jax.experimental import pallas as pl
from jax.experimental.pallas import tpu as pltpu
from jax.sharding import PartitionSpec as P

BLOCK = 128


damping = 0.1


def rotate_rows(rows, grad_blocks):
    row_count = rows.shape[0]
    nblocks = grad_blocks.shape[0]
    block_width = grad_blocks.shape[1]
    reshaped = rows.reshape(row_count, nblocks, block_width)
    turned = jnp.einsum("tcg,cgh->tch", reshaped, grad_blocks, preferred_element_type=jnp.float32)
    return turned.astype(jnp.bfloat16).reshape(row_count, nblocks * block_width)


def pick_scores(totals, block_tokens, pair_query, pair_block):
    blocks = block_tokens.reshape(-1, BLOCK)
    picked = jnp.take(totals, pair_query, axis=0)
    token_ids = jnp.take(blocks, pair_block, axis=0)
    return jnp.take_along_axis(picked, token_ids, axis=1)


def by_columns(
    query_grads,
    eigen_values,
    act_basis,
    grad_basis,
    activations,
    cotangents,
    block_tokens,
    pair_query,
    pair_block,
):
    grad_full = lax.all_gather(grad_basis, "tensor", axis=0, tiled=True)
    block_width = grad_full.shape[1]
    model_cols = grad_full.shape[0]
    grad_blocks = grad_full.reshape(model_cols // block_width, block_width, block_width)
    act_local = lax.all_to_all(activations, "tensor", split_axis=1, concat_axis=0, tiled=True)
    tokens_all = act_local.shape[0]
    slice_cols = act_local.shape[1]
    owned_blocks = act_basis.shape[0]
    act_size = act_basis.shape[1]
    act_rot = jnp.einsum(
        "tkb,kbc->tkc",
        act_local.reshape(tokens_all, owned_blocks, act_size),
        act_basis,
        preferred_element_type=jnp.float32,
    )
    act_rot = act_rot.astype(jnp.bfloat16).reshape(tokens_all, slice_cols)
    cot_mine = rotate_rows(cotangents, grad_blocks)
    cot_rot = lax.all_gather(cot_mine, "tensor", axis=0, tiled=True)
    query_piece = lax.all_to_all(query_grads, "tensor", split_axis=2, concat_axis=1, tiled=True)
    number = query_piece.shape[0]
    turned = jnp.einsum(
        "nokb,kbc->nokc",
        query_piece.reshape(number, model_cols, owned_blocks, act_size),
        act_basis,
        preferred_element_type=jnp.float32,
    ).astype(jnp.bfloat16)
    turned = turned.reshape(number, model_cols // block_width, block_width, slice_cols)
    rotated = jnp.einsum("cgh,ncgf->nchf", grad_blocks, turned, preferred_element_type=jnp.float32)
    rotated = rotated.reshape(number, model_cols, slice_cols)
    precond = (rotated / (eigen_values + damping)).astype(jnp.bfloat16)
    act_wide = act_rot.astype(jnp.float32)

    def score_query(matrix):
        values = jnp.dot(cot_rot, matrix, preferred_element_type=jnp.float32)
        return jnp.sum(values * act_wide, axis=1)

    totals = lax.map(score_query, precond)
    return lax.psum(pick_scores(totals, block_tokens, pair_query, pair_block), "tensor")


CHIPS = 16
PLANE = 4


def fused_kernel(
    query_hbm,
    eigen_hbm,
    basis_hbm,
    grad_hbm,
    act_in,
    cot_in,
    out_ref,
    eigen,
    inverse_out,
    inverse_in,
    query,
    rotated,
    act,
    basis,
    grad,
    act_pair,
    cot_mine,
    cot_pair,
    cot,
    sums,
    pair_sums,
    all_sums,
    eigen_sem,
    local_sem,
    query_local,
    query_send,
    query_recv,
    pair_send,
    pair_recv,
    inverse_send,
    inverse_recv,
    act_send,
    act_recv,
    basis_send,
    basis_recv,
    cot_send,
    cot_recv,
    sums_send,
    sums_recv,
):
    bf16, f32 = jnp.bfloat16, jnp.float32
    me = lax.axis_index("tensor")
    core = lax.rem(me, 2)
    chip = me // 2
    z = chip // PLANE
    y = lax.rem(chip // 2, 2)
    x = lax.rem(chip, 2)
    number, rows = query_hbm.shape[0], query_hbm.shape[1]
    width = eigen_hbm.shape[1]
    wide = 2 * rows
    half = CHIPS * width
    tokens = act_in.shape[1]
    both = 2 * tokens
    size = basis_hbm.shape[1]

    def device(at_chip, at_core):
        return {"tensor": 2 * at_chip + at_core}

    def remote(src, dst, send, recv, to):
        return pltpu.make_async_remote_copy(
            src_ref=src,
            dst_ref=dst,
            send_sem=send,
            recv_sem=recv,
            device_id=to,
            device_id_type=pl.DeviceIdType.MESH,
        )

    other = device(chip, 1 - core)

    def nth(step):
        return lax.rem(chip + step, CHIPS)

    def eigen_load(c):
        return pltpu.make_async_copy(eigen_hbm.at[pl.ds(c * wide, wide), :], eigen.at[c], eigen_sem.at[c])

    def query_load(c):
        columns = pl.ds(pl.multiple_of((2 * c + core) * width, width), width)
        mine = pl.ds(pl.multiple_of(core * rows, rows), rows)
        return pltpu.make_async_copy(query_hbm.at[:, :, columns], query.at[c, :, mine, :], query_local.at[c])

    def query_pass(c):
        columns = pl.ds(pl.multiple_of((2 * c + 1 - core) * width, width), width)
        mine = pl.ds(pl.multiple_of(core * rows, rows), rows)
        return remote(query_hbm.at[:, :, columns], query.at[c, :, mine, :], query_send.at[c], query_recv.at[c], other)

    @pl.loop(0, CHIPS)
    def _(step):
        eigen_load(nth(step)).start()

    grad_rows = pl.ds(pl.multiple_of(core * rows, rows), rows)
    grad_load = pltpu.make_async_copy(grad_hbm, grad.at[grad_rows, :], local_sem.at[0])
    grad_load.start()
    basis_load = pltpu.make_async_copy(basis_hbm, basis.at[chip], local_sem.at[1])
    basis_load.start()

    barrier = pltpu.get_barrier_semaphore()
    pl.semaphore_signal(barrier, inc=1, device_id=other, device_id_type=pl.DeviceIdType.MESH)

    @pl.loop(1, CHIPS)
    def _(step):
        pl.semaphore_signal(
            barrier, inc=1, device_id=device(nth(step), core), device_id_type=pl.DeviceIdType.MESH
        )

    pl.semaphore_wait(barrier, CHIPS)

    act_pass = remote(act_in.at[1 - core], act_pair, pair_send.at[0], pair_recv.at[0], other)
    cot_pass = remote(cot_in, cot_pair, pair_send.at[1], pair_recv.at[1], other)
    grad_pass = remote(grad_hbm, grad.at[grad_rows, :], pair_send.at[2], pair_recv.at[2], other)
    act_pass.start()
    cot_pass.start()
    grad_pass.start()

    x_to = device(z * PLANE + y * 2 + 1 - x, core)
    y_to = device(z * PLANE + (1 - y) * 2 + x, core)

    def act_rows(c):
        return act.at[pl.ds(pl.multiple_of(c * both, both), both), :]

    def act_copy(c, way, to):
        return remote(act_rows(c), act_rows(c), act_send.at[way, c], act_recv.at[c], to)

    def basis_copy(c, way, to):
        return remote(basis.at[c], basis.at[c], basis_send.at[way, c], basis_recv.at[c], to)

    def spread(copy, c):
        copy(c, 0, x_to).start()
        copy(c, 1, y_to).start()

    def up(copy, c):
        @pl.when(z < CHIPS // PLANE - 1)
        def _():
            copy(c, 2, device(chip + PLANE, core)).start()

    def down(copy, c):
        @pl.when(z > 0)
        def _():
            copy(c, 3, device(chip - PLANE, core)).start()

    basis_load.wait()
    up(basis_copy, chip)
    down(basis_copy, chip)

    act_pass.wait_recv()

    def join(first, second):
        return jnp.concatenate([first, second], axis=0).astype(bf16)

    @pl.when(core == 0)
    def _():
        act_rows(chip)[...] = join(act_in[0], act_pair[...])

    @pl.when(core == 1)
    def _():
        act_rows(chip)[...] = join(act_pair[...], act_in[1])

    up(act_copy, chip)
    down(act_copy, chip)
    spread(basis_copy, chip)
    spread(act_copy, chip)

    def inverse_copy(c):
        return remote(
            inverse_out.at[c], inverse_in.at[chip], inverse_send.at[c], inverse_recv.at[chip], device(c, core)
        )

    def inverse_arrival(c):
        return remote(inverse_out.at[c], inverse_in.at[c], inverse_send.at[c], inverse_recv.at[c], other)

    @pl.loop(1, CHIPS)
    def _(step):
        c = nth(step)
        eigen_load(c).wait()
        inverse_out[c] = (1.0 / (eigen[c] + damping)).astype(bf16)
        inverse_copy(c).start()

    @pl.loop(0, CHIPS)
    def _(step):
        query_load(nth(step)).start()
        query_pass(nth(step)).start()

    eigen_load(chip).wait()
    inverse_in[chip] = (1.0 / (eigen[chip] + damping)).astype(bf16)

    cot_pass.wait_recv()

    @pl.when(core == 0)
    def _():
        cot_mine[...] = join(cot_in[...], cot_pair[...])

    @pl.when(core == 1)
    def _():
        cot_mine[...] = join(cot_pair[...], cot_in[...])

    def cot_columns(c):
        return cot_mine.at[:, pl.ds(pl.multiple_of(c * wide, wide), wide)]

    def cot_rows(c):
        return cot.at[pl.ds(pl.multiple_of(c * both, both), both), :]

    def cot_copy(c):
        return remote(cot_columns(c), cot_rows(chip), cot_send.at[c], cot_recv.at[chip], device(c, core))

    def cot_arrival(c):
        return remote(cot_columns(c), cot_rows(c), cot_send.at[c], cot_recv.at[c], other)

    @pl.loop(1, CHIPS)
    def _(step):
        cot_copy(nth(step)).start()

    cot_rows(chip)[...] = cot_columns(chip)[...]

    levels = CHIPS // PLANE
    for step in range(1, levels):
        @pl.when(z >= step)
        def _():
            c = chip - step * PLANE
            for copy in (basis_copy, act_copy):
                copy(c, 0, x_to).wait_recv()
                up(copy, c)
                spread(copy, c)

        @pl.when(z + step < levels)
        def _():
            c = chip + step * PLANE
            for copy in (basis_copy, act_copy):
                copy(c, 0, x_to).wait_recv()
                down(copy, c)
                spread(copy, c)

    def level(step):
        return lax.rem(z + step, levels) * PLANE

    def at_x(step):
        return level(step) + y * 2 + 1 - x

    def at_y(step):
        return level(step) + (1 - y) * 2 + x

    def at_both(step):
        return level(step) + (1 - y) * 2 + 1 - x

    @pl.loop(0, levels)
    def _(step):
        basis_copy(at_x(step), 0, x_to).wait_recv()
        act_copy(at_x(step), 0, x_to).wait_recv()
        act_copy(at_x(step), 1, y_to).start()
        act_copy(at_y(step), 0, x_to).wait_recv()
        basis_copy(at_y(step), 0, x_to).wait_recv()
        basis_copy(at_y(step), 0, x_to).start()

    grad_load.wait()
    grad_pass.wait_recv()

    def turn(values, c):
        parts = [
            jnp.dot(
                values[:, k * size:(k + 1) * size],
                basis[c, k * size:(k + 1) * size, :],
                preferred_element_type=f32,
            )
            for k in range(width // size)
        ]
        return jnp.concatenate(parts, axis=1).astype(bf16)

    def rotate(c):
        query_load(c).wait()
        query_pass(c).wait_recv()
        for q in range(number):
            rotated[c, q] = lax.dot_general(
                grad[...], turn(query[c, q], c), (((0,), (0,)), ((), ())), preferred_element_type=f32
            )

    @pl.loop(0, levels)
    def _(step):
        rotate(level(step) + y * 2 + x)
        rotate(at_x(step))
        rotate(at_y(step))

    @pl.loop(0, levels)
    def _(step):
        basis_copy(at_both(step), 0, x_to).wait_recv()
        rotate(at_both(step))
        act_copy(at_both(step), 0, x_to).wait_recv()

    sums[...] = jnp.zeros_like(sums)

    def score(c):
        columns = pl.ds(pl.multiple_of(c * width, width), width)
        act_rot = turn(act[:, columns], c)
        scale = inverse_in[c].astype(f32)
        for q in range(number):
            precond = (rotated[c, q] * scale).astype(bf16)
            sums[q] += lax.dot_general(precond, act_rot, (((1,), (1,)), ((), ())), preferred_element_type=f32)

    score(chip)

    @pl.loop(1, CHIPS)
    def _(step):
        c = lax.rem(chip + CHIPS - step, CHIPS)
        inverse_arrival(c).wait_recv()
        score(c)

    @pl.loop(1, CHIPS)
    def _(step):
        cot_arrival(nth(step)).wait_recv()

    cot_rot = lax.dot_general(grad[...], cot[...], (((0,), (1,)), ((), ())), preferred_element_type=f32)
    cot_rot = cot_rot.astype(bf16).astype(f32)
    for q in range(number):
        pair_sums[core, q:q + 1, :] = jnp.sum(sums[q] * cot_rot, axis=0, keepdims=True)

    core_copy = remote(pair_sums.at[core], pair_sums.at[core], pair_send.at[3], pair_recv.at[3], other)
    core_copy.start()
    core_copy.wait()
    all_sums[chip] = pair_sums[0] + pair_sums[1]

    def sums_copy(c):
        return remote(all_sums.at[chip], all_sums.at[chip], sums_send.at[c], sums_recv.at[chip], device(c, core))

    def sums_arrival(c):
        return remote(all_sums.at[c], all_sums.at[c], sums_send.at[c], sums_recv.at[c], other)

    @pl.loop(1, CHIPS)
    def _(step):
        sums_copy(nth(step)).start()

    act_pass.wait_send()
    cot_pass.wait_send()
    grad_pass.wait_send()

    @pl.loop(0, CHIPS)
    def _(step):
        query_pass(nth(step)).wait_send()

    @pl.loop(1, CHIPS)
    def _(step):
        inverse_copy(nth(step)).wait_send()
        cot_copy(nth(step)).wait_send()

    for copy in (basis_copy, act_copy):
        for step in range(levels):
            c = level(step) + y * 2 + x
            copy(c, 0, x_to).wait_send()
            copy(c, 1, y_to).wait_send()
        for step in range(levels):
            @pl.when((z >= step) & (z < levels - 1))
            def _():
                copy(chip - step * PLANE, 2, x_to).wait_send()

            @pl.when((z + step < levels) & (z > 0))
            def _():
                copy(chip + step * PLANE, 3, x_to).wait_send()

    @pl.loop(0, levels)
    def _(step):
        act_copy(at_x(step), 1, y_to).wait_send()
        basis_copy(at_y(step), 0, x_to).wait_send()

    @pl.loop(1, CHIPS)
    def _(step):
        sums_arrival(nth(step)).wait_recv()

    @pl.loop(1, CHIPS)
    def _(step):
        sums_copy(nth(step)).wait_send()

    out_ref[...] = jnp.sum(all_sums[...], axis=0)


def by_rows(
    query_grads,
    eigen_values,
    act_basis,
    grad_basis,
    activations,
    cotangents,
    block_tokens,
    pair_query,
    pair_block,
):
    bf16, f32 = jnp.bfloat16, jnp.float32
    number, rows, hidden = query_grads.shape
    features, width = eigen_values.shape
    wide = 2 * rows
    half = hidden // 2
    tokens = activations.shape[0]
    all_tokens = 2 * CHIPS * tokens
    blocks, size, _ = act_basis.shape

    act = activations.reshape(tokens, CHIPS, 2, width).transpose(2, 0, 1, 3).reshape(2, tokens, half).astype(f32)
    cot = cotangents.astype(f32)
    vmem, dma = pltpu.VMEM, pltpu.SemaphoreType.DMA
    totals = pl.pallas_call(
        fused_kernel,
        out_shape=jax.ShapeDtypeStruct((number, all_tokens), f32),
        in_specs=[pl.BlockSpec(memory_space=pl.ANY)] * 4 + [pl.BlockSpec(memory_space=pltpu.VMEM)] * 2,
        out_specs=pl.BlockSpec(memory_space=pltpu.VMEM),
        scratch_shapes=[
            vmem((CHIPS, wide, width), f32),
            vmem((CHIPS, wide, width), bf16),
            vmem((CHIPS, wide, width), bf16),
            vmem((CHIPS, number, wide, width), bf16),
            vmem((CHIPS, number, wide, width), f32),
            vmem((all_tokens, half), bf16),
            vmem((CHIPS, blocks * size, size), bf16),
            vmem((wide, wide), bf16),
            vmem((tokens, half), f32),
            vmem((2 * tokens, features), bf16),
            vmem((tokens, features), f32),
            vmem((all_tokens, wide), bf16),
            vmem((number, wide, all_tokens), f32),
            vmem((2, number, all_tokens), f32),
            vmem((CHIPS, number, all_tokens), f32),
            dma((CHIPS,)),
            dma((2,)),
            dma((CHIPS,)),
            dma((CHIPS,)),
            dma((CHIPS,)),
            dma((4,)),
            dma((4,)),
            dma((CHIPS,)),
            dma((CHIPS,)),
            dma((4, CHIPS)),
            dma((CHIPS,)),
            dma((4, CHIPS)),
            dma((CHIPS,)),
            dma((CHIPS,)),
            dma((CHIPS,)),
            dma((CHIPS,)),
            dma((CHIPS,)),
        ],
        compiler_params=pltpu.CompilerParams(
            collective_id=0, has_side_effects=True, vmem_limit_bytes=60 * 1024 * 1024
        ),
        cost_estimate=pl.CostEstimate(flops=7 * 10**9, bytes_accessed=24 * 10**6, transcendentals=0),
    )(query_grads, eigen_values, act_basis.reshape(blocks * size, size), grad_basis, act, cot)
    in_order = jnp.where(block_tokens[None, :, None] == jnp.arange(all_tokens)[None, None, :], totals[:, None, :], 0.0)
    in_order = jnp.sum(in_order, axis=2).reshape(number, -1, BLOCK)
    listed = (pair_query[:, None, None] == jnp.arange(number)[None, :, None]) & (
        pair_block[:, None, None] == jnp.arange(in_order.shape[1])[None, None, :]
    )
    return jnp.sum(jnp.where(listed[..., None], in_order[None], 0.0), axis=(1, 2))


def solution(mesh):
    devices = mesh.shape["tensor"]

    def per_device(*args):
        query_grads, grad_basis = args[0], args[3]
        paired = devices == 2 * CHIPS and 2 * query_grads.shape[1] == grad_basis.shape[1]
        return (by_rows if paired else by_columns)(*args)

    return jax.shard_map(
        per_device,
        mesh=mesh,
        in_specs=(
            P("groups", "tensor", None),
            P("groups", "tensor"),
            P(("groups", "tensor"), None, None),
            P(("groups", "tensor"), None),
            P(("groups", "tensor"), None),
            P(("groups", "tensor"), None),
            P("groups"),
            P("groups"),
            P("groups"),
        ),
        out_specs=P("groups", None),
        check_vma=False,
    )
```

```python
import jax
import jax.numpy as jnp
from jax import lax
from jax.experimental import pallas as pl
from jax.experimental.pallas import tpu as pltpu
from jax.sharding import PartitionSpec as P

BLOCK = 128


damping = 0.1


def rotate_rows(rows, grad_blocks):
    row_count = rows.shape[0]
    nblocks = grad_blocks.shape[0]
    block_width = grad_blocks.shape[1]
    reshaped = rows.reshape(row_count, nblocks, block_width)
    turned = jnp.einsum("tcg,cgh->tch", reshaped, grad_blocks, preferred_element_type=jnp.float32)
    return turned.astype(jnp.bfloat16).reshape(row_count, nblocks * block_width)


def pick_scores(totals, block_tokens, pair_query, pair_block):
    blocks = block_tokens.reshape(-1, BLOCK)
    picked = jnp.take(totals, pair_query, axis=0)
    token_ids = jnp.take(blocks, pair_block, axis=0)
    return jnp.take_along_axis(picked, token_ids, axis=1)


def by_columns(
    query_grads,
    eigen_values,
    act_basis,
    grad_basis,
    activations,
    cotangents,
    block_tokens,
    pair_query,
    pair_block,
):
    grad_full = lax.all_gather(grad_basis, "tensor", axis=0, tiled=True)
    block_width = grad_full.shape[1]
    model_cols = grad_full.shape[0]
    grad_blocks = grad_full.reshape(model_cols // block_width, block_width, block_width)
    act_local = lax.all_to_all(activations, "tensor", split_axis=1, concat_axis=0, tiled=True)
    tokens_all = act_local.shape[0]
    slice_cols = act_local.shape[1]
    owned_blocks = act_basis.shape[0]
    act_size = act_basis.shape[1]
    act_rot = jnp.einsum(
        "tkb,kbc->tkc",
        act_local.reshape(tokens_all, owned_blocks, act_size),
        act_basis,
        preferred_element_type=jnp.float32,
    )
    act_rot = act_rot.astype(jnp.bfloat16).reshape(tokens_all, slice_cols)
    cot_mine = rotate_rows(cotangents, grad_blocks)
    cot_rot = lax.all_gather(cot_mine, "tensor", axis=0, tiled=True)
    query_piece = lax.all_to_all(query_grads, "tensor", split_axis=2, concat_axis=1, tiled=True)
    number = query_piece.shape[0]
    turned = jnp.einsum(
        "nokb,kbc->nokc",
        query_piece.reshape(number, model_cols, owned_blocks, act_size),
        act_basis,
        preferred_element_type=jnp.float32,
    ).astype(jnp.bfloat16)
    turned = turned.reshape(number, model_cols // block_width, block_width, slice_cols)
    rotated = jnp.einsum("cgh,ncgf->nchf", grad_blocks, turned, preferred_element_type=jnp.float32)
    rotated = rotated.reshape(number, model_cols, slice_cols)
    precond = (rotated / (eigen_values + damping)).astype(jnp.bfloat16)
    act_wide = act_rot.astype(jnp.float32)

    def score_query(matrix):
        values = jnp.dot(cot_rot, matrix, preferred_element_type=jnp.float32)
        return jnp.sum(values * act_wide, axis=1)

    totals = lax.map(score_query, precond)
    return lax.psum(pick_scores(totals, block_tokens, pair_query, pair_block), "tensor")


PLANES = 4
PLANE = 8
CHIPS = PLANES * PLANE // 2


def fused_kernel(
    query_hbm,
    eigen_hbm,
    basis_hbm,
    grad_hbm,
    act_in,
    cot_in,
    out_ref,
    eigen,
    inverse_out,
    inverse_in,
    query,
    rotated,
    act_plane,
    act,
    act_rot,
    basis,
    grad,
    cot_line,
    cot,
    sums,
    plane_sums,
    line_sums,
    eigen_sem,
    local_sem,
    query_local,
    query_send,
    query_recv,
    inverse_send,
    inverse_recv,
    plane_send,
    plane_recv,
    act_send,
    act_recv,
    basis_send,
    basis_recv,
    line_send,
    line_recv,
):
    bf16, f32 = jnp.bfloat16, jnp.float32
    me = lax.axis_index("tensor")
    z = me // PLANE
    place = lax.rem(me, PLANE)
    number, rows = query_hbm.shape[0], query_hbm.shape[1]
    width = eigen_hbm.shape[1]
    wide = 2 * rows
    blocks = PLANE // 2
    tokens = act_in.shape[1]
    flock = PLANE * tokens
    size = basis_hbm.shape[1]

    def remote(src, dst, send, recv, to):
        return pltpu.make_async_remote_copy(
            src_ref=src,
            dst_ref=dst,
            send_sem=send,
            recv_sem=recv,
            device_id={"tensor": to},
            device_id_type=pl.DeviceIdType.MESH,
        )

    def in_plane(step):
        return lax.rem(place + step, PLANE)

    def in_line(step):
        return lax.rem(z + step, PLANES)

    def at_place(p):
        return z * PLANE + p

    def at_level(level):
        return level * PLANE + place

    a_plane = at_place(in_plane(1))
    a_line = at_level(in_line(1))

    def eigen_load(c):
        return pltpu.make_async_copy(eigen_hbm.at[pl.ds(c * wide, wide), :], eigen.at[c], eigen_sem.at[c])

    def mine(of):
        return pl.ds(pl.multiple_of(of * rows, rows), rows)

    def query_columns(j, p):
        return query_hbm.at[:, :, pl.ds(pl.multiple_of((j * PLANE + p) * width, width), width)]

    def query_load(j):
        return pltpu.make_async_copy(query_columns(j, place), query.at[j, :, mine(place), :], query_local.at[j])

    def query_copy(j, p):
        return remote(
            query_columns(j, p), query.at[j, :, mine(place), :], query_send.at[j, p], query_recv.at[j, place], at_place(p)
        )

    def query_arrival(j, p):
        return remote(
            query_columns(j, p), query.at[j, :, mine(p), :], query_send.at[j, p], query_recv.at[j, p], a_plane
        )

    @pl.loop(0, PLANES)
    def _(step):
        for b in range(blocks):
            eigen_load(in_line(step + 1) * blocks + b).start()

    grad_load = pltpu.make_async_copy(grad_hbm, grad.at[mine(place), :], local_sem.at[0])
    grad_load.start()
    basis_load = pltpu.make_async_copy(basis_hbm, basis.at[z], local_sem.at[1])
    basis_load.start()

    barrier = pltpu.get_barrier_semaphore()
    for step in range(1, PLANE):
        pl.semaphore_signal(
            barrier, inc=1, device_id={"tensor": at_place(in_plane(step))}, device_id_type=pl.DeviceIdType.MESH
        )
    for step in range(1, PLANES):
        pl.semaphore_signal(
            barrier, inc=1, device_id={"tensor": at_level(in_line(step))}, device_id_type=pl.DeviceIdType.MESH
        )
    pl.semaphore_wait(barrier, PLANE + PLANES - 2)

    def act_copy(p):
        return remote(act_in.at[p], act_plane.at[place], plane_send.at[0, p], plane_recv.at[0, place], at_place(p))

    def act_arrival(p):
        return remote(act_in.at[p], act_plane.at[p], plane_send.at[0, p], plane_recv.at[0, p], a_plane)

    def grad_copy(p):
        return remote(grad_hbm, grad.at[mine(place), :], plane_send.at[1, p], plane_recv.at[1, place], at_place(p))

    def grad_arrival(p):
        return remote(grad_hbm, grad.at[mine(p), :], plane_send.at[1, p], plane_recv.at[1, p], a_plane)

    def cot_copy(level):
        return remote(cot_in.at[level], cot_line.at[z], line_send.at[0, level], line_recv.at[0, z], at_level(level))

    def cot_arrival(level):
        return remote(cot_in.at[level], cot_line.at[level], line_send.at[0, level], line_recv.at[0, level], a_line)

    @pl.loop(1, PLANE)
    def _(step):
        act_copy(in_plane(step)).start()

    for step in range(1, PLANES):
        cot_copy(in_line(step)).start()

    @pl.loop(1, PLANE)
    def _(step):
        grad_copy(in_plane(step)).start()

    act_plane[place] = act_in[place]
    cot_line[z] = cot_in[z]

    def act_rows(level):
        return act.at[pl.ds(pl.multiple_of(level * flock, flock), flock), :]

    def act_hop(level, way, to):
        return remote(act_rows(level), act_rows(level), act_send.at[way, level], act_recv.at[level], to)

    def basis_hop(level, way, to):
        return remote(basis.at[level], basis.at[level], basis_send.at[way, level], basis_recv.at[level], to)

    def up(hop, level):
        @pl.when(z < PLANES - 1)
        def _():
            hop(level, 0, me + PLANE).start()

    def down(hop, level):
        @pl.when(z > 0)
        def _():
            hop(level, 1, me - PLANE).start()

    def pass_on(step):
        @pl.when(z >= step)
        def _():
            for hop in (basis_hop, act_hop):
                hop(z - step, 0, a_line).wait_recv()
                up(hop, z - step)

        @pl.when(z + step < PLANES)
        def _():
            for hop in (basis_hop, act_hop):
                hop(z + step, 0, a_line).wait_recv()
                down(hop, z + step)

    basis_load.wait()
    up(basis_hop, z)
    down(basis_hop, z)

    def inverse_copy(level, b):
        c = level * blocks + b
        return remote(
            inverse_out.at[c],
            inverse_in.at[z * blocks + b],
            inverse_send.at[c],
            inverse_recv.at[z * blocks + b],
            at_level(level),
        )

    def inverse_arrival(level, b):
        c = level * blocks + b
        return remote(inverse_out.at[c], inverse_in.at[c], inverse_send.at[c], inverse_recv.at[c], a_line)

    def invert(step, start, stop):
        @pl.loop(start, stop)
        def _(b):
            c = in_line(step) * blocks + b
            eigen_load(c).wait()
            inverse_out[c] = (1.0 / (eigen[c] + damping)).astype(bf16)
            inverse_copy(in_line(step), b).start()

    def send_query(j):
        query_load(j).start()

        @pl.loop(1, PLANE)
        def _(step):
            query_copy(j, in_plane(step)).start()

    invert(1, 0, 2)
    send_query(z)
    invert(1, 2, blocks)

    @pl.loop(1, PLANE)
    def _(step):
        act_arrival(in_plane(step)).wait_recv()

    act_rows(z)[...] = jnp.concatenate([act_plane[p] for p in range(PLANE)], axis=0).astype(bf16)
    up(act_hop, z)
    down(act_hop, z)

    send_query(in_line(1))
    invert(2, 0, blocks)
    send_query(in_line(2))

    def cot_spread(p):
        return remote(cot.at[place], cot.at[place], plane_send.at[2, p], plane_recv.at[2, place], at_place(p))

    def cot_spread_arrival(p):
        return remote(cot.at[p], cot.at[p], plane_send.at[2, p], plane_recv.at[2, p], a_plane)

    for step in range(1, PLANES):
        cot_arrival(in_line(step)).wait_recv()
    cot[place] = jnp.concatenate([cot_line[level] for level in range(PLANES)], axis=0).astype(bf16)

    @pl.loop(1, PLANE)
    def _(step):
        cot_spread(in_plane(step)).start()

    invert(3, 0, blocks)
    send_query(in_line(3))

    @pl.loop(0, blocks)
    def _(b):
        c = z * blocks + b
        eigen_load(c).wait()
        inverse_in[c] = (1.0 / (eigen[c] + damping)).astype(bf16)

    grad_load.wait()

    @pl.loop(1, PLANE)
    def _(step):
        grad_arrival(in_plane(step)).wait_recv()

    def turn(values, j):
        parts = [
            jnp.dot(
                values[:, k * size:(k + 1) * size],
                basis[j, k * size:(k + 1) * size, :],
                preferred_element_type=f32,
            )
            for k in range(width // size)
        ]
        return jnp.concatenate(parts, axis=1).astype(bf16)

    def grad_block(b):
        return grad[pl.ds(pl.multiple_of(b * wide, wide), wide), :]

    def rotate(j):
        query_load(j).wait()

        @pl.loop(1, PLANE)
        def _(step):
            query_arrival(j, in_plane(step)).wait_recv()

        @pl.loop(0, blocks)
        def _(b):
            these = pl.ds(pl.multiple_of(b * wide, wide), wide)
            for q in range(number):
                rotated[j * blocks + b, q] = lax.dot_general(
                    grad_block(b), turn(query[j, q, these, :], j), (((0,), (0,)), ((), ())), preferred_element_type=f32
                )

    pass_on(1)
    rotate(z)
    pass_on(2)
    pass_on(3)

    @pl.loop(1, PLANES)
    def _(step):
        rotate(in_line(step))

    @pl.loop(0, PLANES)
    def _(j):
        act_rot[j] = turn(act[:, pl.ds(pl.multiple_of(j * width, width), width)], j)

    sums[...] = jnp.zeros_like(sums)

    def score(j, b):
        c = j * blocks + b
        scale = inverse_in[c].astype(f32)
        for q in range(number):
            precond = (rotated[c, q] * scale).astype(bf16)
            sums[b, q] += lax.dot_general(precond, act_rot[j], (((1,), (1,)), ((), ())), preferred_element_type=f32)

    @pl.loop(0, blocks)
    def _(b):
        score(z, b)

    @pl.loop(1, PLANE)
    def _(step):
        cot_spread_arrival(in_plane(step)).wait_recv()

    wide_cot = cot[...].astype(f32)
    pieces = [
        wide_cot[p, level * tokens:(level + 1) * tokens, :] for level in range(PLANES) for p in range(PLANE)
    ]
    cot_rows = jnp.concatenate(pieces, axis=0).astype(bf16)

    @pl.loop(1, PLANES)
    def _(step):
        level = lax.rem(z + PLANES - step, PLANES)

        @pl.loop(0, blocks)
        def _(b):
            inverse_arrival(level, b).wait_recv()
            score(level, b)

    totals = [jnp.zeros((1, sums.shape[3]), f32) for _ in range(number)]
    for b in range(blocks):
        cot_rot = lax.dot_general(
            grad[b * wide:(b + 1) * wide, :],
            cot_rows[:, b * wide:(b + 1) * wide],
            (((0,), (1,)), ((), ())),
            preferred_element_type=f32,
        )
        cot_rot = cot_rot.astype(bf16).astype(f32)
        for q in range(number):
            totals[q] = totals[q] + jnp.sum(sums[b, q] * cot_rot, axis=0, keepdims=True)
    plane_sums[place] = jnp.concatenate(totals, axis=0)

    def plane_copy(p):
        return remote(
            plane_sums.at[place], plane_sums.at[place], plane_send.at[3, p], plane_recv.at[3, place], at_place(p)
        )

    def plane_arrival(p):
        return remote(plane_sums.at[p], plane_sums.at[p], plane_send.at[3, p], plane_recv.at[3, p], a_plane)

    def line_copy(level):
        return remote(line_sums.at[z], line_sums.at[z], line_send.at[1, level], line_recv.at[1, z], at_level(level))

    def line_arrival(level):
        return remote(line_sums.at[level], line_sums.at[level], line_send.at[1, level], line_recv.at[1, level], a_line)

    @pl.loop(1, PLANE)
    def _(step):
        plane_copy(in_plane(step)).start()

    for step in range(1, PLANES):
        cot_copy(in_line(step)).wait_send()
        for b in range(blocks):
            inverse_copy(in_line(step), b).wait_send()

    @pl.loop(1, PLANE)
    def _(step):
        p = in_plane(step)
        act_copy(p).wait_send()
        grad_copy(p).wait_send()
        cot_spread(p).wait_send()
        for j in range(PLANES):
            query_copy(j, p).wait_send()

    for hop in (basis_hop, act_hop):
        for step in range(PLANES):
            @pl.when((z >= step) & (z < PLANES - 1))
            def _():
                hop(z - step, 0, a_line).wait_send()

            @pl.when((z + step < PLANES) & (z > 0))
            def _():
                hop(z + step, 1, a_line).wait_send()

    @pl.loop(1, PLANE)
    def _(step):
        plane_arrival(in_plane(step)).wait_recv()

    line_sums[z] = jnp.sum(plane_sums[...], axis=0)
    for step in range(1, PLANES):
        line_copy(in_line(step)).start()

    @pl.loop(1, PLANE)
    def _(step):
        plane_copy(in_plane(step)).wait_send()

    for step in range(1, PLANES):
        line_arrival(in_line(step)).wait_recv()
    for step in range(1, PLANES):
        line_copy(in_line(step)).wait_send()
    out_ref[...] = jnp.sum(line_sums[...], axis=0)


def by_rows(
    query_grads,
    eigen_values,
    act_basis,
    grad_basis,
    activations,
    cotangents,
    block_tokens,
    pair_query,
    pair_block,
):
    bf16, f32 = jnp.bfloat16, jnp.float32
    number, rows, hidden = query_grads.shape
    features, width = eigen_values.shape
    wide = 2 * rows
    tokens = activations.shape[0]
    all_tokens = 2 * CHIPS * tokens
    blocks, size, _ = act_basis.shape

    split = (tokens, PLANES, PLANE, width)
    act = activations.reshape(split).transpose(2, 0, 1, 3).reshape(PLANE, tokens, PLANES * width).astype(f32)
    cot = cotangents.reshape(tokens, PLANES, -1).transpose(1, 0, 2).astype(f32)
    vmem, dma = pltpu.VMEM, pltpu.SemaphoreType.DMA
    totals = pl.pallas_call(
        fused_kernel,
        out_shape=jax.ShapeDtypeStruct((number, all_tokens), f32),
        in_specs=[pl.BlockSpec(memory_space=pl.ANY)] * 4 + [pl.BlockSpec(memory_space=pltpu.VMEM)] * 2,
        out_specs=pl.BlockSpec(memory_space=pltpu.VMEM),
        scratch_shapes=[
            vmem((CHIPS, wide, width), f32),
            vmem((CHIPS, wide, width), bf16),
            vmem((CHIPS, wide, width), bf16),
            vmem((PLANES, number, PLANE * rows, width), bf16),
            vmem((CHIPS, number, wide, width), f32),
            vmem((PLANE, tokens, PLANES * width), f32),
            vmem((all_tokens, PLANES * width), bf16),
            vmem((PLANES, all_tokens, width), bf16),
            vmem((PLANES, blocks * size, size), bf16),
            vmem((PLANE * rows, wide), bf16),
            vmem((PLANES, tokens, features // PLANES), f32),
            vmem((PLANE, PLANES * tokens, features // PLANES), bf16),
            vmem((PLANE // 2, number, wide, all_tokens), f32),
            vmem((PLANE, number, all_tokens), f32),
            vmem((PLANES, number, all_tokens), f32),
            dma((CHIPS,)),
            dma((2,)),
            dma((PLANES,)),
            dma((PLANES, PLANE)),
            dma((PLANES, PLANE)),
            dma((CHIPS,)),
            dma((CHIPS,)),
            dma((4, PLANE)),
            dma((4, PLANE)),
            dma((2, PLANES)),
            dma((PLANES,)),
            dma((2, PLANES)),
            dma((PLANES,)),
            dma((2, PLANES)),
            dma((2, PLANES)),
        ],
        compiler_params=pltpu.CompilerParams(
            collective_id=0, has_side_effects=True, vmem_limit_bytes=60 * 1024 * 1024
        ),
        cost_estimate=pl.CostEstimate(flops=7 * 10**9, bytes_accessed=24 * 10**6, transcendentals=0),
    )(query_grads, eigen_values, act_basis.reshape(blocks * size, size), grad_basis, act, cot)
    in_order = jnp.where(block_tokens[None, :, None] == jnp.arange(all_tokens)[None, None, :], totals[:, None, :], 0.0)
    in_order = jnp.sum(in_order, axis=2).reshape(number, -1, BLOCK)
    listed = (pair_query[:, None, None] == jnp.arange(number)[None, :, None]) & (
        pair_block[:, None, None] == jnp.arange(in_order.shape[1])[None, None, :]
    )
    return jnp.sum(jnp.where(listed[..., None], in_order[None], 0.0), axis=(1, 2))


def solution(mesh):
    devices = mesh.shape["tensor"]

    def per_device(*args):
        query_grads, grad_basis = args[0], args[3]
        paired = devices == 2 * CHIPS and 2 * query_grads.shape[1] == grad_basis.shape[1]
        return (by_rows if paired else by_columns)(*args)

    return jax.shard_map(
        per_device,
        mesh=mesh,
        in_specs=(
            P("groups", "tensor", None),
            P("groups", "tensor"),
            P(("groups", "tensor"), None, None),
            P(("groups", "tensor"), None),
            P(("groups", "tensor"), None),
            P(("groups", "tensor"), None),
            P("groups"),
            P("groups"),
            P("groups"),
        ),
        out_specs=P("groups", None),
        check_vma=False,
    )
```

```python
import jax
import jax.numpy as jnp
from jax import lax
from jax.experimental import pallas as pl
from jax.experimental.pallas import tpu as pltpu
from jax.sharding import PartitionSpec as P

BLOCK = 128


damping = 0.1


def rotate_rows(rows, grad_blocks):
    row_count = rows.shape[0]
    nblocks = grad_blocks.shape[0]
    block_width = grad_blocks.shape[1]
    reshaped = rows.reshape(row_count, nblocks, block_width)
    turned = jnp.einsum("tcg,cgh->tch", reshaped, grad_blocks, preferred_element_type=jnp.float32)
    return turned.astype(jnp.bfloat16).reshape(row_count, nblocks * block_width)


def pick_scores(totals, block_tokens, pair_query, pair_block):
    blocks = block_tokens.reshape(-1, BLOCK)
    picked = jnp.take(totals, pair_query, axis=0)
    token_ids = jnp.take(blocks, pair_block, axis=0)
    return jnp.take_along_axis(picked, token_ids, axis=1)


def by_columns(
    query_grads,
    eigen_values,
    act_basis,
    grad_basis,
    activations,
    cotangents,
    block_tokens,
    pair_query,
    pair_block,
):
    grad_full = lax.all_gather(grad_basis, "tensor", axis=0, tiled=True)
    block_width = grad_full.shape[1]
    model_cols = grad_full.shape[0]
    grad_blocks = grad_full.reshape(model_cols // block_width, block_width, block_width)
    act_local = lax.all_to_all(activations, "tensor", split_axis=1, concat_axis=0, tiled=True)
    tokens_all = act_local.shape[0]
    slice_cols = act_local.shape[1]
    owned_blocks = act_basis.shape[0]
    act_size = act_basis.shape[1]
    act_rot = jnp.einsum(
        "tkb,kbc->tkc",
        act_local.reshape(tokens_all, owned_blocks, act_size),
        act_basis,
        preferred_element_type=jnp.float32,
    )
    act_rot = act_rot.astype(jnp.bfloat16).reshape(tokens_all, slice_cols)
    cot_mine = rotate_rows(cotangents, grad_blocks)
    cot_rot = lax.all_gather(cot_mine, "tensor", axis=0, tiled=True)
    query_piece = lax.all_to_all(query_grads, "tensor", split_axis=2, concat_axis=1, tiled=True)
    number = query_piece.shape[0]
    turned = jnp.einsum(
        "nokb,kbc->nokc",
        query_piece.reshape(number, model_cols, owned_blocks, act_size),
        act_basis,
        preferred_element_type=jnp.float32,
    ).astype(jnp.bfloat16)
    turned = turned.reshape(number, model_cols // block_width, block_width, slice_cols)
    rotated = jnp.einsum("cgh,ncgf->nchf", grad_blocks, turned, preferred_element_type=jnp.float32)
    rotated = rotated.reshape(number, model_cols, slice_cols)
    precond = (rotated / (eigen_values + damping)).astype(jnp.bfloat16)
    act_wide = act_rot.astype(jnp.float32)

    def score_query(matrix):
        values = jnp.dot(cot_rot, matrix, preferred_element_type=jnp.float32)
        return jnp.sum(values * act_wide, axis=1)

    totals = lax.map(score_query, precond)
    return lax.psum(pick_scores(totals, block_tokens, pair_query, pair_block), "tensor")


PLANES = 4
PLANE = 8
CHIPS = PLANES * PLANE // 2


def fused_kernel(
    query_hbm,
    eigen_hbm,
    basis_hbm,
    grad_hbm,
    act_in,
    cot_in,
    out_ref,
    eigen,
    inverse_out,
    inverse_in,
    query,
    rotated,
    act_plane,
    act,
    act_rot,
    basis,
    grad,
    cot_line,
    cot,
    cot_rot,
    sums,
    plane_sums,
    line_sums,
    eigen_sem,
    local_sem,
    query_local,
    query_send,
    query_recv,
    inverse_send,
    inverse_recv,
    plane_send,
    plane_recv,
    act_send,
    act_recv,
    basis_send,
    basis_recv,
    line_send,
    line_recv,
):
    bf16, f32 = jnp.bfloat16, jnp.float32
    me = lax.axis_index("tensor")
    z = me // PLANE
    place = lax.rem(me, PLANE)
    number, rows = query_hbm.shape[0], query_hbm.shape[1]
    width = eigen_hbm.shape[1]
    wide = 2 * rows
    blocks = PLANE // 2
    tokens = act_in.shape[1]
    flock = PLANE * tokens
    size = basis_hbm.shape[1]

    def remote(src, dst, send, recv, to):
        return pltpu.make_async_remote_copy(
            src_ref=src,
            dst_ref=dst,
            send_sem=send,
            recv_sem=recv,
            device_id={"tensor": to},
            device_id_type=pl.DeviceIdType.MESH,
        )

    def in_plane(step):
        return lax.rem(place + step, PLANE)

    def in_line(step):
        return lax.rem(z + step, PLANES)

    def at_place(p):
        return z * PLANE + p

    def at_level(level):
        return level * PLANE + place

    a_plane = at_place(in_plane(1))
    a_line = at_level(in_line(1))

    def eigen_load(c):
        return pltpu.make_async_copy(eigen_hbm.at[pl.ds(c * wide, wide), :], eigen.at[c], eigen_sem.at[c])

    def mine(of):
        return pl.ds(pl.multiple_of(of * rows, rows), rows)

    def query_columns(j, p):
        return query_hbm.at[:, :, pl.ds(pl.multiple_of((j * PLANE + p) * width, width), width)]

    def query_load(j):
        return pltpu.make_async_copy(query_columns(j, place), query.at[j, :, mine(place), :], query_local.at[j])

    def query_copy(j, p):
        return remote(
            query_columns(j, p), query.at[j, :, mine(place), :], query_send.at[j, p], query_recv.at[j, place], at_place(p)
        )

    def query_arrival(j, p):
        return remote(
            query_columns(j, p), query.at[j, :, mine(p), :], query_send.at[j, p], query_recv.at[j, p], a_plane
        )

    @pl.loop(0, PLANES)
    def _(step):
        for b in range(blocks):
            eigen_load(in_line(step + 1) * blocks + b).start()

    grad_load = pltpu.make_async_copy(grad_hbm, grad.at[mine(place), :], local_sem.at[0])
    grad_load.start()
    basis_load = pltpu.make_async_copy(basis_hbm, basis.at[z], local_sem.at[1])
    basis_load.start()

    barrier = pltpu.get_barrier_semaphore()
    for step in range(1, PLANE):
        pl.semaphore_signal(
            barrier, inc=1, device_id={"tensor": at_place(in_plane(step))}, device_id_type=pl.DeviceIdType.MESH
        )
    for step in range(1, PLANES):
        pl.semaphore_signal(
            barrier, inc=1, device_id={"tensor": at_level(in_line(step))}, device_id_type=pl.DeviceIdType.MESH
        )
    pl.semaphore_wait(barrier, PLANE + PLANES - 2)

    def act_copy(p):
        return remote(act_in.at[p], act_plane.at[place], plane_send.at[0, p], plane_recv.at[0, place], at_place(p))

    def act_arrival(p):
        return remote(act_in.at[p], act_plane.at[p], plane_send.at[0, p], plane_recv.at[0, p], a_plane)

    def grad_copy(p):
        return remote(grad_hbm, grad.at[mine(place), :], plane_send.at[1, p], plane_recv.at[1, place], at_place(p))

    def grad_arrival(p):
        return remote(grad_hbm, grad.at[mine(p), :], plane_send.at[1, p], plane_recv.at[1, p], a_plane)

    def cot_copy(level):
        return remote(cot_in.at[level], cot_line.at[z], line_send.at[0, level], line_recv.at[0, z], at_level(level))

    def cot_arrival(level):
        return remote(cot_in.at[level], cot_line.at[level], line_send.at[0, level], line_recv.at[0, level], a_line)

    @pl.loop(1, PLANE)
    def _(step):
        act_copy(in_plane(step)).start()

    for step in range(1, PLANES):
        cot_copy(in_line(step)).start()

    @pl.loop(1, PLANE)
    def _(step):
        grad_copy(in_plane(step)).start()

    act_plane[place] = act_in[place]
    cot_line[z] = cot_in[z]

    def act_rows(level):
        return act.at[pl.ds(pl.multiple_of(level * flock, flock), flock), :]

    def act_hop(level, way, to):
        return remote(act_rows(level), act_rows(level), act_send.at[way, level], act_recv.at[level], to)

    def basis_hop(level, way, to):
        return remote(basis.at[level], basis.at[level], basis_send.at[way, level], basis_recv.at[level], to)

    def up(hop, level):
        @pl.when(z < PLANES - 1)
        def _():
            hop(level, 0, me + PLANE).start()

    def down(hop, level):
        @pl.when(z > 0)
        def _():
            hop(level, 1, me - PLANE).start()

    def pass_on(step):
        @pl.when(z >= step)
        def _():
            for hop in (basis_hop, act_hop):
                hop(z - step, 0, a_line).wait_recv()
                up(hop, z - step)

        @pl.when(z + step < PLANES)
        def _():
            for hop in (basis_hop, act_hop):
                hop(z + step, 0, a_line).wait_recv()
                down(hop, z + step)

    basis_load.wait()
    up(basis_hop, z)
    down(basis_hop, z)

    def inverse_copy(level, b):
        c = level * blocks + b
        return remote(
            inverse_out.at[c],
            inverse_in.at[z * blocks + b],
            inverse_send.at[c],
            inverse_recv.at[z * blocks + b],
            at_level(level),
        )

    def inverse_arrival(level, b):
        c = level * blocks + b
        return remote(inverse_out.at[c], inverse_in.at[c], inverse_send.at[c], inverse_recv.at[c], a_line)

    def invert(step, start, stop):
        @pl.loop(start, stop)
        def _(b):
            c = in_line(step) * blocks + b
            eigen_load(c).wait()
            inverse_out[c] = (1.0 / (eigen[c] + damping)).astype(bf16)
            inverse_copy(in_line(step), b).start()

    def send_query(j):
        query_load(j).start()

        @pl.loop(1, PLANE)
        def _(step):
            query_copy(j, in_plane(step)).start()

    invert(2, 0, 2)
    send_query(z)

    @pl.loop(1, PLANE)
    def _(step):
        act_arrival(in_plane(step)).wait_recv()

    act_rows(z)[...] = jnp.concatenate([act_plane[p] for p in range(PLANE)], axis=0).astype(bf16)
    up(act_hop, z)
    down(act_hop, z)

    invert(2, 2, blocks)
    send_query(in_line(PLANES - 2))
    invert(1, 0, blocks)
    pass_on(1)
    send_query(in_line(PLANES - 1))

    def cot_spread(p):
        return remote(cot.at[place], cot.at[place], plane_send.at[2, p], plane_recv.at[2, place], at_place(p))

    def cot_spread_arrival(p):
        return remote(cot.at[p], cot.at[p], plane_send.at[2, p], plane_recv.at[2, p], a_plane)

    for step in range(1, PLANES):
        cot_arrival(in_line(step)).wait_recv()
    cot[place] = jnp.concatenate([cot_line[level] for level in range(PLANES)], axis=0).astype(bf16)

    @pl.loop(1, PLANE)
    def _(step):
        cot_spread(in_plane(step)).start()

    invert(3, 0, blocks)
    send_query(in_line(PLANES - 3))
    pass_on(2)

    @pl.loop(0, blocks)
    def _(b):
        c = z * blocks + b
        eigen_load(c).wait()
        inverse_in[c] = (1.0 / (eigen[c] + damping)).astype(bf16)

    grad_load.wait()

    @pl.loop(1, PLANE)
    def _(step):
        grad_arrival(in_plane(step)).wait_recv()

    def turn(values, j):
        parts = [
            jnp.dot(
                values[:, k * size:(k + 1) * size],
                basis[j, k * size:(k + 1) * size, :],
                preferred_element_type=f32,
            )
            for k in range(width // size)
        ]
        return jnp.concatenate(parts, axis=1).astype(bf16)

    def grad_block(b):
        return grad[pl.ds(pl.multiple_of(b * wide, wide), wide), :]

    def rotate(j):
        query_load(j).wait()

        @pl.loop(1, PLANE)
        def _(step):
            query_arrival(j, in_plane(step)).wait_recv()

        @pl.loop(0, blocks)
        def _(b):
            these = pl.ds(pl.multiple_of(b * wide, wide), wide)
            for q in range(number):
                rotated[j * blocks + b, q] = lax.dot_general(
                    grad_block(b), turn(query[j, q, these, :], j), (((0,), (0,)), ((), ())), preferred_element_type=f32
                )

    sums[...] = jnp.zeros_like(sums)

    def score(j, b):
        c = j * blocks + b
        scale = inverse_in[c].astype(f32)
        for q in range(number):
            precond = (rotated[c, q] * scale).astype(bf16)
            sums[b, q] += lax.dot_general(precond, act_rot[j], (((1,), (1,)), ((), ())), preferred_element_type=f32)

    rotate(z)
    pass_on(3)

    @pl.loop(0, PLANES)
    def _(j):
        act_rot[j] = turn(act[:, pl.ds(pl.multiple_of(j * width, width), width)], j)

    @pl.loop(0, blocks)
    def _(b):
        score(z, b)

    def rotate_and_score(step):
        level = lax.rem(z + PLANES - step, PLANES)
        rotate(level)

        @pl.loop(0, blocks)
        def _(b):
            inverse_arrival(level, b).wait_recv()
            score(level, b)

    @pl.loop(1, PLANES - 1)
    def _(step):
        rotate_and_score(PLANES - 1 - step)

    @pl.loop(1, PLANE)
    def _(step):
        cot_spread_arrival(in_plane(step)).wait_recv()

    wide_cot = cot[...].astype(f32)
    pieces = [
        wide_cot[p, level * tokens:(level + 1) * tokens, :] for level in range(PLANES) for p in range(PLANE)
    ]
    cot_rows = jnp.concatenate(pieces, axis=0).astype(bf16)
    for b in range(blocks):
        cot_rot[b] = lax.dot_general(
            grad[b * wide:(b + 1) * wide, :],
            cot_rows[:, b * wide:(b + 1) * wide],
            (((0,), (1,)), ((), ())),
            preferred_element_type=f32,
        ).astype(bf16).astype(f32)
    rotate_and_score(PLANES - 1)

    totals = [jnp.zeros((1, sums.shape[3]), f32) for _ in range(number)]
    for b in range(blocks):
        for q in range(number):
            totals[q] = totals[q] + jnp.sum(sums[b, q] * cot_rot[b], axis=0, keepdims=True)
    plane_sums[place] = jnp.concatenate(totals, axis=0)

    def plane_copy(p):
        return remote(
            plane_sums.at[place], plane_sums.at[place], plane_send.at[3, p], plane_recv.at[3, place], at_place(p)
        )

    def plane_arrival(p):
        return remote(plane_sums.at[p], plane_sums.at[p], plane_send.at[3, p], plane_recv.at[3, p], a_plane)

    def line_copy(level):
        return remote(line_sums.at[z], line_sums.at[z], line_send.at[1, level], line_recv.at[1, z], at_level(level))

    def line_arrival(level):
        return remote(line_sums.at[level], line_sums.at[level], line_send.at[1, level], line_recv.at[1, level], a_line)

    @pl.loop(1, PLANE)
    def _(step):
        plane_copy(in_plane(step)).start()

    for step in range(1, PLANES):
        cot_copy(in_line(step)).wait_send()
        for b in range(blocks):
            inverse_copy(in_line(step), b).wait_send()

    @pl.loop(1, PLANE)
    def _(step):
        p = in_plane(step)
        act_copy(p).wait_send()
        grad_copy(p).wait_send()
        cot_spread(p).wait_send()
        for j in range(PLANES):
            query_copy(j, p).wait_send()

    for hop in (basis_hop, act_hop):
        for step in range(PLANES):
            @pl.when((z >= step) & (z < PLANES - 1))
            def _():
                hop(z - step, 0, a_line).wait_send()

            @pl.when((z + step < PLANES) & (z > 0))
            def _():
                hop(z + step, 1, a_line).wait_send()

    @pl.loop(1, PLANE)
    def _(step):
        plane_arrival(in_plane(step)).wait_recv()

    line_sums[z] = jnp.sum(plane_sums[...], axis=0)
    for step in range(1, PLANES):
        line_copy(in_line(step)).start()

    @pl.loop(1, PLANE)
    def _(step):
        plane_copy(in_plane(step)).wait_send()

    for step in range(1, PLANES):
        line_arrival(in_line(step)).wait_recv()
    for step in range(1, PLANES):
        line_copy(in_line(step)).wait_send()
    out_ref[...] = jnp.sum(line_sums[...], axis=0)


def by_rows(
    query_grads,
    eigen_values,
    act_basis,
    grad_basis,
    activations,
    cotangents,
    block_tokens,
    pair_query,
    pair_block,
):
    bf16, f32 = jnp.bfloat16, jnp.float32
    number, rows, hidden = query_grads.shape
    features, width = eigen_values.shape
    wide = 2 * rows
    tokens = activations.shape[0]
    all_tokens = 2 * CHIPS * tokens
    blocks, size, _ = act_basis.shape

    split = (tokens, PLANES, PLANE, width)
    act = activations.reshape(split).transpose(2, 0, 1, 3).reshape(PLANE, tokens, PLANES * width).astype(f32)
    cot = cotangents.reshape(tokens, PLANES, -1).transpose(1, 0, 2).astype(f32)
    vmem, dma = pltpu.VMEM, pltpu.SemaphoreType.DMA
    totals = pl.pallas_call(
        fused_kernel,
        out_shape=jax.ShapeDtypeStruct((number, all_tokens), f32),
        in_specs=[pl.BlockSpec(memory_space=pl.ANY)] * 4 + [pl.BlockSpec(memory_space=pltpu.VMEM)] * 2,
        out_specs=pl.BlockSpec(memory_space=pltpu.VMEM),
        scratch_shapes=[
            vmem((CHIPS, wide, width), f32),
            vmem((CHIPS, wide, width), bf16),
            vmem((CHIPS, wide, width), bf16),
            vmem((PLANES, number, PLANE * rows, width), bf16),
            vmem((CHIPS, number, wide, width), f32),
            vmem((PLANE, tokens, PLANES * width), f32),
            vmem((all_tokens, PLANES * width), bf16),
            vmem((PLANES, all_tokens, width), bf16),
            vmem((PLANES, blocks * size, size), bf16),
            vmem((PLANE * rows, wide), bf16),
            vmem((PLANES, tokens, features // PLANES), f32),
            vmem((PLANE, PLANES * tokens, features // PLANES), bf16),
            vmem((PLANE // 2, wide, all_tokens), f32),
            vmem((PLANE // 2, number, wide, all_tokens), f32),
            vmem((PLANE, number, all_tokens), f32),
            vmem((PLANES, number, all_tokens), f32),
            dma((CHIPS,)),
            dma((2,)),
            dma((PLANES,)),
            dma((PLANES, PLANE)),
            dma((PLANES, PLANE)),
            dma((CHIPS,)),
            dma((CHIPS,)),
            dma((4, PLANE)),
            dma((4, PLANE)),
            dma((2, PLANES)),
            dma((PLANES,)),
            dma((2, PLANES)),
            dma((PLANES,)),
            dma((2, PLANES)),
            dma((2, PLANES)),
        ],
        compiler_params=pltpu.CompilerParams(
            collective_id=0, has_side_effects=True, vmem_limit_bytes=60 * 1024 * 1024
        ),
        cost_estimate=pl.CostEstimate(flops=7 * 10**9, bytes_accessed=24 * 10**6, transcendentals=0),
    )(query_grads, eigen_values, act_basis.reshape(blocks * size, size), grad_basis, act, cot)
    in_order = jnp.where(block_tokens[None, :, None] == jnp.arange(all_tokens)[None, None, :], totals[:, None, :], 0.0)
    in_order = jnp.sum(in_order, axis=2).reshape(number, -1, BLOCK)
    listed = (pair_query[:, None, None] == jnp.arange(number)[None, :, None]) & (
        pair_block[:, None, None] == jnp.arange(in_order.shape[1])[None, None, :]
    )
    return jnp.sum(jnp.where(listed[..., None], in_order[None], 0.0), axis=(1, 2))


def solution(mesh):
    devices = mesh.shape["tensor"]

    def per_device(*args):
        query_grads, grad_basis = args[0], args[3]
        paired = devices == 2 * CHIPS and 2 * query_grads.shape[1] == grad_basis.shape[1]
        return (by_rows if paired else by_columns)(*args)

    return jax.shard_map(
        per_device,
        mesh=mesh,
        in_specs=(
            P("groups", "tensor", None),
            P("groups", "tensor"),
            P(("groups", "tensor"), None, None),
            P(("groups", "tensor"), None),
            P(("groups", "tensor"), None),
            P(("groups", "tensor"), None),
            P("groups"),
            P("groups"),
            P("groups"),
        ),
        out_specs=P("groups", None),
        check_vma=False,
    )
```
